32 devices in a mesh: dp: 8 (over y, x, core), tensor: 4 (over z).
Axes of the slice: x: 2, y: 2, z: 4, core: 2. Of those that a mesh axis runs over, the one named last changes fastest.
Arguments:
- token_ids: int32 [4096], P('dp'), may hold values from 0 to 511
- table: bfloat16 [512, 2560], replicated, may hold values from -27 to 27
- weights: bfloat16 [2560, 10240], P(None, 'tensor'), may hold values from -6 to 6
- targets: bfloat16 [4096, 10240], P('dp', 'tensor'), may hold values from -5.5 to 5.5
- momentum: float32 [2560, 10240], P('dp', 'tensor'), may hold values from -6 to 6
Outputs:
- new_weights: bfloat16 [2560, 10240], P(None, 'tensor')
- new_momentum: float32 [2560, 10240], P('dp', 'tensor')
The draws below stay inside these ranges and needn't reach their ends.
All inputs are finite; a program needn't handle non-finite values.
Results may differ from the reference program's by a relative error of at most 0.0052.
Values may be sent and summed in bfloat16 or wider, within the bound.
A program may use at most 128 MiB of HBM per device.

```python
import math
import jax
import jax.numpy as jnp
import numpy as np
from jax import lax

D = 2560
FF = 10240
TOK_DEV = 512
TABLE_ROWS = 512
TOKENS = 4096
LEVELS = 3
N_DP = 8


def draw_table(key, part):
    base_key, factor_key = jax.random.split(key)
    base_draw = jax.random.truncated_normal(base_key, -3.0, 3.0, (TABLE_ROWS, D), jnp.float32)
    block_scale = jnp.ones((TABLE_ROWS, N_DP), jnp.float32)
    for tree_level in range(LEVELS):
        group_total = 2 ** (tree_level + 1)
        exponent = jax.random.uniform(jax.random.fold_in(factor_key, tree_level + 17), (TABLE_ROWS, group_total), jnp.float32, -1.0, 1.0)
        level_factor = jnp.exp(exponent * 1.0986123) / 1.4223
        block_scale = block_scale * jnp.repeat(level_factor, N_DP // group_total, axis=1)
    block_scale = jnp.repeat(block_scale, D // N_DP, axis=1)
    return (base_draw * block_scale / math.sqrt(D)).astype(jnp.bfloat16)


def draw_targets(key, part):
    noise_key = jax.random.fold_in(key, 101)
    noise = jax.random.truncated_normal(noise_key, -4.0, 4.0, (TOKENS, FF), jnp.float32)
    replica = jnp.arange(TOKENS, dtype=jnp.int32) // TOK_DEV
    column_block = jnp.arange(FF, dtype=jnp.int32) * 4 // FF
    flips = replica[:, None] & column_block[None, :] & 3
    parity = flips & 1 ^ flips >> 1
    offset = 1.5 * (1.0 - 2.0 * parity.astype(jnp.float32))
    return (noise + offset).astype(jnp.bfloat16)


def place_ends(array, rng, smallest, largest):
    longest = array.shape.index(max(array.shape))
    spots = []
    for shift in (0, 1):
        where = [jax.random.randint(jax.random.fold_in(rng, axis), (), 0, length) for axis, length in enumerate(array.shape)]
        where[longest] = (where[longest] + shift) % array.shape[longest]
        spots.append(tuple(where))
    return array.at[spots[0]].set(smallest).at[spots[1]].set(largest)


def shard_levels(key, dims, cuts, least, top_value):
    loudness = 1.0
    for dim, shards_of in cuts:
        steps = jax.random.uniform(jax.random.fold_in(jax.random.fold_in(key, 6), dim), (shards_of,), jnp.float32, least / len(cuts), top_value / len(cuts))
        loudness = loudness * jnp.repeat(jnp.exp(steps), dims[dim] // shards_of).reshape((-1,) + (1,) * (len(dims) - 1 - dim))
    return loudness


def rank_bounds(number_of, skew):
    weights = [(1 << 20) // math.isqrt(grade ** skew) + 1 for grade in range(1, number_of + 1)]
    spread = 1 + sum(weights) // (1 << 30)
    return np.cumsum(np.array([max(1, weight // spread) for weight in weights]))


def ranked_ids(key, extent, amount, slope):
    grid = rank_bounds(amount, slope)
    lot = jax.random.randint(jax.random.fold_in(key, 1), extent, 0, int(grid[amount - 1]))
    rank = jnp.searchsorted(jnp.asarray(grid, jnp.int32), lot, side="right")
    return jax.random.permutation(jax.random.fold_in(key, 2), amount)[rank].astype(jnp.int32)


def bell_draw(own_key, shape, deviation, bound, cuts=(), kind=jnp.bfloat16):
    values = deviation * jax.random.normal(own_key, shape, jnp.float32)
    if cuts:
        values = values * shard_levels(own_key, shape, cuts, -0.22, 0.18)
    return jnp.clip(values, -bound, bound).astype(kind)


def setup_inputs(seed: int = 0) -> dict:
    keys = jax.random.split(jax.random.key(seed), 6)
    token_ids = place_ends(ranked_ids(keys[0], (TOKENS,), TABLE_ROWS, 2), jax.random.fold_in(keys[0], 3), 0, TABLE_ROWS - 1).astype(jnp.int32)
    table = draw_table(jax.random.fold_in(keys[5], 71), 0)
    weights = bell_draw(keys[2], (D, FF), 1.0, 6.0, ((1, 4),))
    targets = draw_targets(jax.random.fold_in(keys[5], 71), 0)
    momentum = bell_draw(keys[4], (D, FF), 1.0, 6.0, ((0, 8), (1, 4)), jnp.float32)
    return {"token_ids": token_ids, "table": table, "weights": weights, "targets": targets, "momentum": momentum}


epsilon = 1e-06
momentum_decay = 0.9
learning_rate = 0.25

def gelu_tanh(values):
    return jax.nn.gelu(values, approximate=True)

def replica_grad(replica_ids, replica_targets, table, weights):
    rows_in = jnp.take(table, replica_ids, axis=0)
    preact = jnp.dot(rows_in, weights, preferred_element_type=jnp.float32)
    activated, pullback = jax.vjp(gelu_tanh, preact)
    grad_pre = pullback(activated - replica_targets.astype(jnp.float32))[0].astype(jnp.bfloat16)
    return lax.dot_general(rows_in, grad_pre, (((0,), (0,)), ((), ())), preferred_element_type=jnp.float32).astype(jnp.bfloat16)

def adasum_pair(first_vec, second_vec):
    first_vec = first_vec.astype(jnp.float32)
    second_vec = second_vec.astype(jnp.float32)
    cross_dot = jnp.sum(first_vec * second_vec)
    first_sq = jnp.sum(first_vec * first_vec)
    second_sq = jnp.sum(second_vec * second_vec)
    return (1.0 - cross_dot / (2.0 * (first_sq + epsilon))) * first_vec + (1.0 - cross_dot / (2.0 * (second_sq + epsilon))) * second_vec

def reference(token_ids, table, weights, targets, momentum):

    def subtree(members, tree_level):
        if len(members) == 1:
            replica = members[0]
            return replica_grad(token_ids[replica * TOK_DEV:(replica + 1) * TOK_DEV], targets[replica * TOK_DEV:(replica + 1) * TOK_DEV], table, weights)
        low_side = [member for member in members if member >> tree_level & 1 == 0]
        high_side = [member for member in members if member >> tree_level & 1 == 1]
        merged = adasum_pair(subtree(low_side, tree_level + 1), subtree(high_side, tree_level + 1))
        if tree_level > 0:
            merged = merged.astype(jnp.bfloat16)
        return merged
    adasum = subtree(list(range(N_DP)), 0)
    new_momentum = momentum_decay * momentum + adasum
    new_weights = (weights.astype(jnp.float32) - learning_rate * new_momentum).astype(jnp.bfloat16)
    return (new_weights, new_momentum)
```

```python
import jax
import jax.numpy as jnp
from jax import lax
from jax.sharding import PartitionSpec as P

epsilon = 1e-06
momentum_decay = 0.9
learning_rate = 0.25


def gelu_tanh(values):
    return jax.nn.gelu(values, approximate=True)


def row_grads(token_ids, table, weights, targets):
    row = lax.broadcasted_iota(jnp.int32, (table.shape[0], token_ids.shape[0]), 0)
    hot = row == token_ids[None, :]
    count = jnp.sum(hot.astype(jnp.float32), axis=1, keepdims=True)
    target_sum = jnp.dot(hot.astype(jnp.bfloat16), targets, preferred_element_type=jnp.float32)
    preact = jnp.dot(table, weights, preferred_element_type=jnp.float32)
    activated, pullback = jax.vjp(gelu_tanh, preact)
    return pullback(count * activated - target_sum)[0].astype(jnp.bfloat16)


def split_kernel(table):
    kern = lax.dot_general(
        table, table, (((1,), (1,)), ((), ())), preferred_element_type=jnp.float32
    )
    high = kern.astype(jnp.bfloat16)
    return high, (kern - high.astype(jnp.float32)).astype(jnp.bfloat16)


def tree_coefficients(gram):
    replicas = gram.shape[0]
    vecs = jnp.eye(replicas, dtype=jnp.float32)
    while vecs.shape[0] > 1:
        half = vecs.shape[0] // 2
        low, high = vecs[:half], vecs[half:]
        low_g = jnp.sum(low[:, :, None] * gram[None], axis=1)
        high_g = jnp.sum(high[:, :, None] * gram[None], axis=1)
        cross = jnp.sum(low_g * high, axis=1, keepdims=True)
        low_sq = jnp.maximum(jnp.sum(low_g * low, axis=1, keepdims=True), 0.0)
        high_sq = jnp.maximum(jnp.sum(high_g * high, axis=1, keepdims=True), 0.0)
        vecs = (1.0 - cross / (2.0 * (low_sq + epsilon))) * low + (
            1.0 - cross / (2.0 * (high_sq + epsilon))
        ) * high
    return vecs[0]


def body(token_ids, table, weights, targets, momentum):
    replicas = lax.axis_size("dp")
    me = lax.axis_index("dp")
    all_momentum = lax.all_gather(momentum.astype(jnp.bfloat16), "dp", axis=0, tiled=True)
    grads = row_grads(token_ids, table, weights, targets)
    rows, cols = grads.shape
    own = lax.all_to_all(grads, "dp", split_axis=1, concat_axis=0, tiled=True)
    own = own.reshape(replicas, rows, cols // replicas)
    high, low = split_kernel(table)
    gram = []
    for other in range(replicas):
        mapped = jnp.dot(high, own[other], preferred_element_type=jnp.float32) + jnp.dot(
            low, own[other], preferred_element_type=jnp.float32
        )
        gram.append(jnp.sum(own.astype(jnp.float32) * mapped[None], axis=(1, 2)))
    gram = lax.psum(jnp.stack(gram), ("dp", "tensor"))
    coefs = tree_coefficients(gram)
    mixed = jnp.sum(own.astype(jnp.float32) * coefs[:, None, None], axis=0).astype(jnp.bfloat16)
    mixed = lax.all_gather(mixed, "dp", axis=1, tiled=True)
    adasum = lax.dot_general(
        table, mixed, (((0,), (0,)), ((), ())), preferred_element_type=jnp.float32
    )
    owned = momentum.shape[0]
    own_table = lax.dynamic_slice_in_dim(table, me * owned, owned, 1)
    own_adasum = lax.dot_general(
        own_table, mixed, (((0,), (0,)), ((), ())), preferred_element_type=jnp.float32
    )
    new_momentum = momentum_decay * momentum + own_adasum
    new_weights = (
        weights.astype(jnp.float32)
        - learning_rate * (momentum_decay * all_momentum.astype(jnp.float32) + adasum)
    ).astype(jnp.bfloat16)
    return (new_weights, new_momentum)


def solution(mesh):
    placed = (P("dp"), P(), P(None, "tensor"), P("dp", "tensor"), P("dp", "tensor"))
    return jax.shard_map(
        body,
        mesh=mesh,
        in_specs=placed,
        out_specs=(P(None, "tensor"), P("dp", "tensor")),
        check_vma=False,
    )
```

```python
import jax
import jax.numpy as jnp
from jax import lax
from jax.experimental import pallas as pl
from jax.experimental.pallas import tpu as pltpu
from jax.sharding import PartitionSpec as P

epsilon = 1e-06
momentum_decay = 0.9
learning_rate = 0.25


def gelu_tanh(values):
    return jax.nn.gelu(values, approximate=True)


def row_grads(token_ids, table, weights, targets):
    row = lax.broadcasted_iota(jnp.int32, (table.shape[0], token_ids.shape[0]), 0)
    hot = row == token_ids[None, :]
    count = jnp.sum(hot.astype(jnp.float32), axis=1, keepdims=True)
    target_sum = jnp.dot(hot.astype(jnp.bfloat16), targets, preferred_element_type=jnp.float32)
    preact = jnp.dot(table, weights, preferred_element_type=jnp.float32)
    activated, pullback = jax.vjp(gelu_tanh, preact)
    return pullback(count * activated - target_sum)[0].astype(jnp.bfloat16)


def split_kernel(table):
    kern = lax.dot_general(
        table, table, (((1,), (1,)), ((), ())), preferred_element_type=jnp.float32
    )
    high = kern.astype(jnp.bfloat16)
    return high, (kern - high.astype(jnp.float32)).astype(jnp.bfloat16)


def tree_coefficients(gram):
    replicas = gram.shape[0]
    vecs = jnp.eye(replicas, dtype=jnp.float32)
    while vecs.shape[0] > 1:
        half = vecs.shape[0] // 2
        low, high = vecs[:half], vecs[half:]
        low_g = jnp.sum(low[:, :, None] * gram[None], axis=1)
        high_g = jnp.sum(high[:, :, None] * gram[None], axis=1)
        cross = jnp.sum(low_g * high, axis=1, keepdims=True)
        low_sq = jnp.maximum(jnp.sum(low_g * low, axis=1, keepdims=True), 0.0)
        high_sq = jnp.maximum(jnp.sum(high_g * high, axis=1, keepdims=True), 0.0)
        vecs = (1.0 - cross / (2.0 * (low_sq + epsilon))) * low + (
            1.0 - cross / (2.0 * (high_sq + epsilon))
        ) * high
    return vecs[0]


def body(token_ids, table, weights, targets, momentum):
    replicas = lax.axis_size("dp")
    me = lax.axis_index("dp")
    all_momentum = lax.all_gather(momentum.astype(jnp.bfloat16), "dp", axis=0, tiled=True)
    grads = row_grads(token_ids, table, weights, targets)
    rows, cols = grads.shape
    own = lax.all_to_all(grads, "dp", split_axis=1, concat_axis=0, tiled=True)
    own = own.reshape(replicas, rows, cols // replicas)
    high, low = split_kernel(table)
    gram = []
    for other in range(replicas):
        mapped = jnp.dot(high, own[other], preferred_element_type=jnp.float32) + jnp.dot(
            low, own[other], preferred_element_type=jnp.float32
        )
        gram.append(jnp.sum(own.astype(jnp.float32) * mapped[None], axis=(1, 2)))
    gram = lax.psum(jnp.stack(gram), ("dp", "tensor"))
    coefs = tree_coefficients(gram)
    mixed = jnp.sum(own.astype(jnp.float32) * coefs[:, None, None], axis=0).astype(jnp.bfloat16)
    mixed = lax.all_gather(mixed, "dp", axis=1, tiled=True)
    adasum = lax.dot_general(
        table, mixed, (((0,), (0,)), ((), ())), preferred_element_type=jnp.float32
    )
    owned = momentum.shape[0]
    own_table = lax.dynamic_slice_in_dim(table, me * owned, owned, 1)
    own_adasum = lax.dot_general(
        own_table, mixed, (((0,), (0,)), ((), ())), preferred_element_type=jnp.float32
    )
    new_momentum = momentum_decay * momentum + own_adasum
    new_weights = (
        weights.astype(jnp.float32)
        - learning_rate * (momentum_decay * all_momentum.astype(jnp.float32) + adasum)
    ).astype(jnp.bfloat16)
    return (new_weights, new_momentum)


MESH = pl.DeviceIdType.MESH


def flip(index, bits):
    out = 0
    for place in (4, 2, 1):
        bit = lax.rem(lax.div(index, place), 2)
        out = out + place * lax.rem(bit + lax.rem(lax.div(bits, place), 2), 2)
    return out


class Gather:
    def __init__(self, me, own, out, send, recv, parts):
        self.me, self.own, self.out, self.send, self.recv = me, own, out, send, recv
        self.parts, self.piece = parts, own.shape[0]
        self.rows = self.piece // parts

    def place(self, owner, part):
        start = pl.multiple_of(owner * self.piece + part * self.rows, 16)
        return self.out.at[pl.ds(start, self.rows)]

    def moved(self, kind, part):
        if kind in (0, 1, 3):
            owner, towards = 0, {0: 2, 1: 4, 3: 1}[kind]
        elif kind == 2:
            owner, towards = (2, 4) if part < self.parts // 2 else (4, 2)
        else:
            owner, towards = {4: 2, 5: 4, 6: 6}[kind], 1
        return owner, towards

    def copy(self, kind, part):
        owner, towards = self.moved(kind, part)
        here = self.place(flip(self.me, owner), part)
        source = self.own.at[pl.ds(part * self.rows, self.rows)] if owner == 0 else here
        return pltpu.make_async_remote_copy(
            src_ref=source,
            dst_ref=here,
            send_sem=self.send.at[kind, part],
            recv_sem=self.recv.at[kind, part],
            device_id={"dp": flip(self.me, towards)},
            device_id_type=MESH,
        )

    def arrived(self, kind, part):
        owner, towards = self.moved(kind, part)
        here = self.place(flip(self.me, owner ^ towards), part)
        pltpu.make_async_remote_copy(
            src_ref=here,
            dst_ref=here,
            send_sem=self.send.at[kind, part],
            recv_sem=self.recv.at[kind, part],
            device_id={"dp": flip(self.me, towards)},
            device_id_type=MESH,
        ).wait_recv()


def exchange(axis, size, value, sent, slots, send, recv):
    me = lax.axis_index(axis)
    sent[...] = value
    slots[me] = value
    copies = []
    for shift in range(1, size):
        copies.append(
            pltpu.make_async_remote_copy(
                src_ref=sent,
                dst_ref=slots.at[me],
                send_sem=send.at[shift],
                recv_sem=recv.at[shift],
                device_id={axis: lax.rem(me + shift, size)},
                device_id_type=MESH,
            )
        )
        copies[-1].start()
    for shift in range(1, size):
        origin = lax.rem(me + size - shift, size)
        pltpu.make_async_remote_copy(
            src_ref=sent,
            dst_ref=slots.at[origin],
            send_sem=send.at[shift],
            recv_sem=recv.at[shift],
            device_id={axis: origin},
            device_id_type=MESH,
        ).wait_recv()
    total = slots[0]
    for index in range(1, size):
        total = total + slots[index]
    return total, copies


def tree_columns(gram):
    rows = lax.broadcasted_iota(jnp.int32, gram.shape, 0)
    lanes = lax.broadcasted_iota(jnp.int32, (1, gram.shape[1]), 1)
    vecs = [
        ((rows == index).astype(jnp.float32), (lanes == index).astype(jnp.float32))
        for index in range(8)
    ]

    def inner(left, right):
        mapped = jnp.sum(left[0] * gram, axis=0, keepdims=True)
        return jnp.broadcast_to(jnp.sum(mapped * right[1], axis=1, keepdims=True), lanes.shape)

    while len(vecs) > 1:
        half = len(vecs) // 2
        merged = []
        for low, high in zip(vecs[:half], vecs[half:]):
            cross = inner(low, high)
            low_sq = jnp.maximum(inner(low, low), 0.0)
            high_sq = jnp.maximum(inner(high, high), 0.0)
            first = 1.0 - cross / (2.0 * (low_sq + epsilon))
            second = 1.0 - cross / (2.0 * (high_sq + epsilon))
            merged.append(
                (first * low[0] + second * high[0], first * low[1] + second * high[1])
            )
        vecs = merged
    return vecs[0][0]


def mix_kernel(
    ids, table, weights, targets, momentum, mix_out, mom_out,
    wbuf, tbuf, gt, gx, kern_high, kern_low, mapped, sums, coef_buf, mix_own,
    t_sent, t_slots, d_sent, d_slots,
    w_sem, t_sem, local_sem, mom_send, mom_recv, mix_send, mix_recv,
    g_send, g_recv, ts_send, ts_recv, ds_send, ds_recv,
):
    me = lax.axis_index("dp")
    mine = lax.axis_index("tensor")
    chip, core = lax.div(me, 2), lax.rem(me, 2)
    width = wbuf.shape[2]
    chunk = gt.shape[1]

    def block(step):
        return lax.div(flip(2 * chip, 2 * lax.rem(step + 1, 4)), 2)

    def fetch(step, slot):
        at = pl.ds(pl.multiple_of(block(step) * width, 128), width)
        return (
            pltpu.make_async_copy(weights.at[:, at], wbuf.at[slot], w_sem.at[slot]),
            pltpu.make_async_copy(targets.at[:, at], tbuf.at[slot], t_sem.at[slot]),
        )

    for load in fetch(0, 0):
        load.start()

    barrier = pltpu.get_barrier_semaphore()
    for shift in range(1, 8):
        pl.semaphore_signal(
            barrier, inc=1, device_id={"dp": lax.rem(me + shift, 8)}, device_id_type=MESH
        )
    for shift in range(1, 4):
        pl.semaphore_signal(
            barrier, inc=1, device_id={"tensor": lax.rem(mine + shift, 4)}, device_id_type=MESH
        )
    pl.semaphore_wait(barrier, 10)

    mom = Gather(me, momentum, mom_out, mom_send, mom_recv, 4)
    mix = Gather(me, mix_own, mix_out, mix_send, mix_recv, 2)
    own_rows = pl.ds(pl.multiple_of(me * mom.piece, 16), mom.piece)
    keep_mom = pltpu.make_async_copy(momentum, mom_out.at[own_rows], local_sem.at[0])
    keep_mom.start()
    for part in (0, 1):
        mom.copy(0, part).start()
        mom.copy(1, part + 2).start()
    for part in range(4):
        mom.copy(3, part).start()

    row = lax.broadcasted_iota(jnp.int32, (table.shape[0], ids.shape[1]), 0)
    hot = (row == ids[...]).astype(jnp.float32)
    count = jnp.sum(hot, axis=1, keepdims=True)
    hot = hot.astype(jnp.bfloat16)

    def sent_grad(step, other):
        bits = 2 * lax.rem(step + 1, 4) + other
        target = flip(me, bits)
        return pltpu.make_async_remote_copy(
            src_ref=gt.at[target],
            dst_ref=gx.at[me],
            send_sem=g_send.at[bits],
            recv_sem=g_recv.at[bits],
            device_id={"dp": target},
            device_id_type=MESH,
        )

    def grads(step, carry):
        slot = lax.rem(step, 2)
        for load in fetch(step, slot):
            load.wait()

        @pl.when(step < 3)
        def _():
            for load in fetch(step + 1, 1 - slot):
                load.start()

        x = jnp.dot(table[...], wbuf[slot], preferred_element_type=jnp.float32)
        target_sum = jnp.dot(hot, tbuf[slot], preferred_element_type=jnp.float32)
        scale = 0.7978845608028654
        square = x * x
        tanh = jnp.tanh(scale * (x + 0.044715 * (square * x)))
        half = 0.5 * (1.0 + tanh)
        slope = half + 0.5 * x * (1.0 - tanh * tanh) * (scale * (1.0 + 3 * 0.044715 * square))
        grad = (slope * (count * (x * half) - target_sum)).T.astype(jnp.bfloat16)
        dest = block(step)
        gt[2 * dest] = grad[:chunk]
        gt[2 * dest + 1] = grad[chunk:]

        @pl.when(step < 3)
        def _():
            sent_grad(step, 0).start()

        sent_grad(step, 1).start()
        return carry

    lax.fori_loop(0, 4, grads, 0)
    gx[me] = gt[me]

    for part in (0, 1):
        mom.copy(1, part).start()
        mom.copy(0, part + 2).start()

    kern = lax.dot_general(
        table[...], table[...], (((1,), (1,)), ((), ())), preferred_element_type=jnp.float32
    )
    high = kern.astype(jnp.bfloat16)
    kern_high[...] = high
    kern_low[...] = (kern - high.astype(jnp.float32)).astype(jnp.bfloat16)

    for part in (0, 1):
        mom.arrived(0, part)
        mom.copy(2, part).start()
        mom.copy(4, part).start()
        mom.arrived(1, part + 2)
        mom.copy(2, part + 2).start()
        mom.copy(5, part + 2).start()

    def grams(bits, carry):
        source = flip(me, bits)

        @pl.when(bits > 0)
        def _():
            pltpu.make_async_remote_copy(
                src_ref=gt.at[source],
                dst_ref=gx.at[source],
                send_sem=g_send.at[bits],
                recv_sem=g_recv.at[bits],
                device_id={"dp": source},
                device_id_type=MESH,
            ).wait_recv()

        mapped[...] = jnp.dot(
            gx[source], kern_high[...], preferred_element_type=jnp.float32
        ) + jnp.dot(gx[source], kern_low[...], preferred_element_type=jnp.float32)

        def pair(other, inner_carry):
            partner = flip(me, other)
            total = jnp.sum(
                gx[partner].astype(jnp.float32) * mapped[...], axis=0, keepdims=True
            )
            sums[source, pl.ds(partner, 1), :] = total
            sums[partner, pl.ds(source, 1), :] = total
            return inner_carry

        lax.fori_loop(0, bits + 1, pair, 0)
        return carry

    lax.fori_loop(0, 8, grams, 0)

    lanes = lax.broadcasted_iota(jnp.int32, (8, 128), 1)
    gram = jnp.zeros((8, 128), jnp.float32)
    for index in range(8):
        column = jnp.sum(sums[index], axis=1, keepdims=True)
        gram = gram + jnp.where(lanes == index, column, 0.0)
    gram, t_copies = exchange("tensor", 4, gram, t_sent, t_slots, ts_send, ts_recv)
    gram, d_copies = exchange("dp", 8, gram, d_sent, d_slots, ds_send, ds_recv)
    coef_buf[...] = tree_columns(gram)

    for lane in range(gx.shape[2] // 128):
        at = pl.ds(lane * 128, 128)
        total = coef_buf[0:1, :] * gx[0, :, at].astype(jnp.float32)
        for index in range(1, 8):
            total = total + coef_buf[index : index + 1, :] * gx[index, :, at].astype(jnp.float32)
        mix_own[:, at] = total.astype(jnp.bfloat16)

    keep_mix = pltpu.make_async_copy(
        mix_own,
        mix_out.at[pl.ds(pl.multiple_of(me * chunk, 16), chunk)],
        local_sem.at[1],
    )
    keep_mix.start()
    mix.copy(0, 0).start()
    mix.copy(1, 1).start()
    mix.copy(0, 1).start()
    mix.copy(1, 0).start()
    for part in (0, 1):
        mix.copy(3, part).start()

    mix.arrived(0, 0)
    mix.copy(2, 0).start()
    mix.copy(4, 0).start()
    mix.arrived(1, 1)
    mix.copy(2, 1).start()
    mix.copy(5, 1).start()
    for part in (0, 1):
        mom.arrived(1, part)
        mom.copy(5, part).start()
        mom.arrived(0, part + 2)
        mom.copy(4, part + 2).start()
    for part in range(4):
        mom.arrived(2, part)
        mom.copy(6, part).start()
    mix.arrived(0, 1)
    mix.copy(4, 1).start()
    mix.arrived(1, 0)
    mix.copy(5, 0).start()
    for part in (0, 1):
        mix.arrived(2, part)
        mix.copy(6, part).start()

    for gather in (mom, mix):
        for part in range(gather.parts):
            for kind in (3, 4, 5, 6):
                gather.arrived(kind, part)
            for kind in range(7):
                gather.copy(kind, part).wait_send()
    for step in range(4):
        if step < 3:
            sent_grad(step, 0).wait_send()
        sent_grad(step, 1).wait_send()
    for copy in t_copies + d_copies:
        copy.wait_send()
    keep_mom.wait()
    keep_mix.wait()


def mixed_grads(token_ids, table, weights, targets, momentum):
    rows, depth = table.shape
    cols = weights.shape[1]
    chunk = cols // 8
    width = 2 * chunk
    anywhere = pl.BlockSpec(memory_space=pl.ANY)
    resident = pl.BlockSpec(memory_space=pltpu.VMEM)
    dma = pltpu.SemaphoreType.DMA
    bf16, f32 = jnp.bfloat16, jnp.float32
    return pl.pallas_call(
        mix_kernel,
        out_shape=(
            jax.ShapeDtypeStruct((cols, rows), bf16),
            jax.ShapeDtypeStruct((8 * momentum.shape[0], cols), bf16),
        ),
        in_specs=[resident, resident, anywhere, anywhere, anywhere],
        out_specs=(anywhere, anywhere),
        scratch_shapes=[
            pltpu.VMEM((2, depth, width), bf16),
            pltpu.VMEM((2, targets.shape[0], width), bf16),
            pltpu.VMEM((8, chunk, rows), bf16),
            pltpu.VMEM((8, chunk, rows), bf16),
            pltpu.VMEM((rows, rows), bf16),
            pltpu.VMEM((rows, rows), bf16),
            pltpu.VMEM((chunk, rows), f32),
            pltpu.VMEM((8, 8, rows), f32),
            pltpu.VMEM((8, 128), f32),
            pltpu.VMEM((chunk, rows), bf16),
            pltpu.VMEM((8, 128), f32),
            pltpu.VMEM((4, 8, 128), f32),
            pltpu.VMEM((8, 128), f32),
            pltpu.VMEM((8, 8, 128), f32),
            dma((2,)), dma((2,)), dma((2,)),
            dma((7, 4)), dma((7, 4)), dma((7, 2)), dma((7, 2)),
            dma((8,)), dma((8,)), dma((4,)), dma((4,)), dma((8,)), dma((8,)),
        ],
        compiler_params=pltpu.CompilerParams(
            collective_id=0, has_side_effects=True, vmem_limit_bytes=56 * 2**20
        ),
        cost_estimate=pl.CostEstimate(
            flops=2 * rows * depth * cols, bytes_accessed=2 * depth * cols, transcendentals=0
        ),
    )(token_ids[None, :], table, weights, targets, momentum)


def update_kernel(table, own_table, mix, weights, all_momentum, momentum, new_weights, new_momentum):
    def spread(columns):
        return lax.dot_general(
            columns.T, mix[...], (((1,), (1,)), ((), ())), preferred_element_type=jnp.float32
        )

    @pl.when(pl.program_id(0) == 0)
    def _():
        new_momentum[...] = momentum_decay * momentum[...] + spread(own_table[...])

    step = momentum_decay * all_momentum[...].astype(jnp.float32) + spread(table[...])
    new_weights[...] = (weights[...].astype(jnp.float32) - learning_rate * step).astype(
        jnp.bfloat16
    )


def updated(table, own_table, mix, weights, all_momentum, momentum):
    rows, depth = table.shape
    cols = weights.shape[1]
    tile = 256
    owned = momentum.shape[0]

    def whole(shape):
        return pl.BlockSpec(shape, lambda step: (0, 0))

    def by_rows():
        return pl.BlockSpec((tile, cols), lambda step: (step, 0))

    return pl.pallas_call(
        update_kernel,
        grid=(depth // tile,),
        out_shape=(
            jax.ShapeDtypeStruct((depth, cols), jnp.bfloat16),
            jax.ShapeDtypeStruct((owned, cols), jnp.float32),
        ),
        in_specs=[
            pl.BlockSpec((rows, tile), lambda step: (0, step)),
            whole((rows, owned)),
            whole((cols, rows)),
            by_rows(),
            by_rows(),
            whole((owned, cols)),
        ],
        out_specs=(by_rows(), whole((owned, cols))),
        compiler_params=pltpu.CompilerParams(vmem_limit_bytes=56 * 2**20),
        cost_estimate=pl.CostEstimate(
            flops=2 * rows * depth * cols, bytes_accessed=6 * depth * cols, transcendentals=0
        ),
    )(table, own_table, mix, weights, all_momentum, momentum)


def kernel_body(token_ids, table, weights, targets, momentum):
    owned = momentum.shape[0]
    mix, all_momentum = mixed_grads(
        token_ids, table, weights, targets, momentum.astype(jnp.bfloat16)
    )
    own_table = lax.dynamic_slice_in_dim(table, lax.axis_index("dp") * owned, owned, 1)
    return updated(table, own_table, mix, weights, all_momentum, momentum)


def solution(mesh):
    placed = (P("dp"), P(), P(None, "tensor"), P("dp", "tensor"), P("dp", "tensor"))
    small = mesh.shape["dp"] == 8 and mesh.shape["tensor"] == 4
    return jax.shard_map(
        kernel_body if small else body,
        mesh=mesh,
        in_specs=placed,
        out_specs=(P(None, "tensor"), P("dp", "tensor")),
        check_vma=False,
    )
```

```python
import jax
import jax.numpy as jnp
from jax import lax
from jax.experimental import pallas as pl
from jax.experimental.pallas import tpu as pltpu
from jax.sharding import PartitionSpec as P

epsilon = 1e-06
momentum_decay = 0.9
learning_rate = 0.25


def gelu_tanh(values):
    return jax.nn.gelu(values, approximate=True)


def row_grads(token_ids, table, weights, targets):
    row = lax.broadcasted_iota(jnp.int32, (table.shape[0], token_ids.shape[0]), 0)
    hot = row == token_ids[None, :]
    count = jnp.sum(hot.astype(jnp.float32), axis=1, keepdims=True)
    target_sum = jnp.dot(hot.astype(jnp.bfloat16), targets, preferred_element_type=jnp.float32)
    preact = jnp.dot(table, weights, preferred_element_type=jnp.float32)
    activated, pullback = jax.vjp(gelu_tanh, preact)
    return pullback(count * activated - target_sum)[0].astype(jnp.bfloat16)


def split_kernel(table):
    kern = lax.dot_general(
        table, table, (((1,), (1,)), ((), ())), preferred_element_type=jnp.float32
    )
    high = kern.astype(jnp.bfloat16)
    return high, (kern - high.astype(jnp.float32)).astype(jnp.bfloat16)


def tree_coefficients(gram):
    replicas = gram.shape[0]
    vecs = jnp.eye(replicas, dtype=jnp.float32)
    while vecs.shape[0] > 1:
        half = vecs.shape[0] // 2
        low, high = vecs[:half], vecs[half:]
        low_g = jnp.sum(low[:, :, None] * gram[None], axis=1)
        high_g = jnp.sum(high[:, :, None] * gram[None], axis=1)
        cross = jnp.sum(low_g * high, axis=1, keepdims=True)
        low_sq = jnp.maximum(jnp.sum(low_g * low, axis=1, keepdims=True), 0.0)
        high_sq = jnp.maximum(jnp.sum(high_g * high, axis=1, keepdims=True), 0.0)
        vecs = (1.0 - cross / (2.0 * (low_sq + epsilon))) * low + (
            1.0 - cross / (2.0 * (high_sq + epsilon))
        ) * high
    return vecs[0]


def body(token_ids, table, weights, targets, momentum):
    replicas = lax.axis_size("dp")
    me = lax.axis_index("dp")
    all_momentum = lax.all_gather(momentum.astype(jnp.bfloat16), "dp", axis=0, tiled=True)
    grads = row_grads(token_ids, table, weights, targets)
    rows, cols = grads.shape
    own = lax.all_to_all(grads, "dp", split_axis=1, concat_axis=0, tiled=True)
    own = own.reshape(replicas, rows, cols // replicas)
    high, low = split_kernel(table)
    gram = []
    for other in range(replicas):
        mapped = jnp.dot(high, own[other], preferred_element_type=jnp.float32) + jnp.dot(
            low, own[other], preferred_element_type=jnp.float32
        )
        gram.append(jnp.sum(own.astype(jnp.float32) * mapped[None], axis=(1, 2)))
    gram = lax.psum(jnp.stack(gram), ("dp", "tensor"))
    coefs = tree_coefficients(gram)
    mixed = jnp.sum(own.astype(jnp.float32) * coefs[:, None, None], axis=0).astype(jnp.bfloat16)
    mixed = lax.all_gather(mixed, "dp", axis=1, tiled=True)
    adasum = lax.dot_general(
        table, mixed, (((0,), (0,)), ((), ())), preferred_element_type=jnp.float32
    )
    owned = momentum.shape[0]
    own_table = lax.dynamic_slice_in_dim(table, me * owned, owned, 1)
    own_adasum = lax.dot_general(
        own_table, mixed, (((0,), (0,)), ((), ())), preferred_element_type=jnp.float32
    )
    new_momentum = momentum_decay * momentum + own_adasum
    new_weights = (
        weights.astype(jnp.float32)
        - learning_rate * (momentum_decay * all_momentum.astype(jnp.float32) + adasum)
    ).astype(jnp.bfloat16)
    return (new_weights, new_momentum)


MESH = pl.DeviceIdType.MESH


def flip(index, bits):
    out = 0
    for place in (4, 2, 1):
        bit = lax.rem(lax.div(index, place), 2)
        out = out + place * lax.rem(bit + lax.rem(lax.div(bits, place), 2), 2)
    return out


class Gather:
    def __init__(self, me, own, out, send, recv, parts):
        self.me, self.own, self.out, self.send, self.recv = me, own, out, send, recv
        self.parts, self.piece = parts, own.shape[0]
        self.rows = self.piece // parts

    def place(self, owner, part):
        start = pl.multiple_of(owner * self.piece + part * self.rows, 16)
        return self.out.at[pl.ds(start, self.rows)]

    def moved(self, kind, part):
        if kind in (0, 1, 3):
            owner, towards = 0, {0: 2, 1: 4, 3: 1}[kind]
        elif kind == 2:
            owner, towards = (2, 4) if part < self.parts // 2 else (4, 2)
        else:
            owner, towards = {4: 2, 5: 4, 6: 6}[kind], 1
        return owner, towards

    def copy(self, kind, part):
        owner, towards = self.moved(kind, part)
        here = self.place(flip(self.me, owner), part)
        source = self.own.at[pl.ds(part * self.rows, self.rows)] if owner == 0 else here
        return pltpu.make_async_remote_copy(
            src_ref=source,
            dst_ref=here,
            send_sem=self.send.at[kind, part],
            recv_sem=self.recv.at[kind, part],
            device_id={"dp": flip(self.me, towards)},
            device_id_type=MESH,
        )

    def arrived(self, kind, part):
        owner, towards = self.moved(kind, part)
        here = self.place(flip(self.me, owner ^ towards), part)
        pltpu.make_async_remote_copy(
            src_ref=here,
            dst_ref=here,
            send_sem=self.send.at[kind, part],
            recv_sem=self.recv.at[kind, part],
            device_id={"dp": flip(self.me, towards)},
            device_id_type=MESH,
        ).wait_recv()


def exchange(axis, size, value, sent, slots, send, recv, meanwhile):
    me = lax.axis_index(axis)
    sent[...] = value
    slots[me] = value
    copies = []
    for shift in range(1, size):
        copies.append(
            pltpu.make_async_remote_copy(
                src_ref=sent,
                dst_ref=slots.at[me],
                send_sem=send.at[shift],
                recv_sem=recv.at[shift],
                device_id={axis: lax.rem(me + shift, size)},
                device_id_type=MESH,
            )
        )
        copies[-1].start()
    meanwhile()
    for shift in range(1, size):
        origin = lax.rem(me + size - shift, size)
        pltpu.make_async_remote_copy(
            src_ref=sent,
            dst_ref=slots.at[origin],
            send_sem=send.at[shift],
            recv_sem=recv.at[shift],
            device_id={axis: origin},
            device_id_type=MESH,
        ).wait_recv()
    total = slots[0]
    for index in range(1, size):
        total = total + slots[index]
    return total, copies


def tree_columns(gram):
    rows = lax.broadcasted_iota(jnp.int32, gram.shape, 0)
    lanes = lax.broadcasted_iota(jnp.int32, (1, gram.shape[1]), 1)
    vecs = [
        ((rows == index).astype(jnp.float32), (lanes == index).astype(jnp.float32))
        for index in range(8)
    ]

    def inner(left, right):
        mapped = jnp.sum(left[0] * gram, axis=0, keepdims=True)
        return jnp.broadcast_to(jnp.sum(mapped * right[1], axis=1, keepdims=True), lanes.shape)

    while len(vecs) > 1:
        half = len(vecs) // 2
        merged = []
        for low, high in zip(vecs[:half], vecs[half:]):
            cross = inner(low, high)
            low_sq = jnp.maximum(inner(low, low), 0.0)
            high_sq = jnp.maximum(inner(high, high), 0.0)
            first = 1.0 - cross / (2.0 * (low_sq + epsilon))
            second = 1.0 - cross / (2.0 * (high_sq + epsilon))
            merged.append(
                (first * low[0] + second * high[0], first * low[1] + second * high[1])
            )
        vecs = merged
    return vecs[0][0]


def mix_kernel(
    ids, table, weights, targets, momentum, mix_out, mom_out, turned_out,
    mom_wide, mom_own, turned, wbuf, tbuf, gt, gx, kern_high, kern_low, mapped, sums, coef_buf, mix_own,
    t_sent, t_slots, d_sent, d_slots,
    w_sem, t_sem, m_sem, local_sem, mom_send, mom_recv, mix_send, mix_recv,
    g_send, g_recv, ts_send, ts_recv, ds_send, ds_recv,
):
    me = lax.axis_index("dp")
    mine = lax.axis_index("tensor")
    chip, core = lax.div(me, 2), lax.rem(me, 2)
    width = wbuf.shape[2]
    chunk = gt.shape[1]

    def block(step):
        return lax.div(flip(2 * chip, 2 * lax.rem(step + 1, 4)), 2)

    def fetch(step, slot):
        at = pl.ds(pl.multiple_of(block(step) * width, 128), width)
        return (
            pltpu.make_async_copy(weights.at[:, at], wbuf.at[slot], w_sem.at[slot]),
            pltpu.make_async_copy(targets.at[:, at], tbuf.at[slot], t_sem.at[slot]),
        )

    mom = Gather(me, mom_own, mom_out, mom_send, mom_recv, 4)
    mix = Gather(me, mix_own, mix_out, mix_send, mix_recv, 2)

    def mom_rows(part):
        return pl.ds(part * mom.rows, mom.rows)

    def mom_load(part):
        at = mom_rows(part)
        return pltpu.make_async_copy(momentum.at[at], mom_wide.at[at], m_sem.at[part])

    for part in (0, 2, 1, 3):
        mom_load(part).start()
    for load in fetch(0, 0):
        load.start()

    barrier = pltpu.get_barrier_semaphore()
    for shift in range(1, 8):
        pl.semaphore_signal(
            barrier, inc=1, device_id={"dp": lax.rem(me + shift, 8)}, device_id_type=MESH
        )
    for shift in range(1, 4):
        pl.semaphore_signal(
            barrier, inc=1, device_id={"tensor": lax.rem(mine + shift, 4)}, device_id_type=MESH
        )
    for part in (0, 2, 1, 3):
        mom_load(part).wait()
        mom_own[mom_rows(part), :] = mom_wide[mom_rows(part), :].astype(jnp.bfloat16)
    pl.semaphore_wait(barrier, 10)

    own_rows = pl.ds(pl.multiple_of(me * mom.piece, 16), mom.piece)
    keep_mom = pltpu.make_async_copy(mom_own, mom_out.at[own_rows], local_sem.at[0])
    keep_mom.start()
    for part in (0, 1):
        mom.copy(0, part).start()
        mom.copy(1, part + 2).start()
    for part in range(4):
        mom.copy(3, part).start()

    row = lax.broadcasted_iota(jnp.int32, (table.shape[0], ids.shape[1]), 0)
    hot = (row == ids[...]).astype(jnp.float32)
    count = jnp.sum(hot, axis=1, keepdims=True)
    hot = hot.astype(jnp.bfloat16)

    def sent_grad(step, other):
        bits = 2 * lax.rem(step + 1, 4) + other
        target = flip(me, bits)
        return pltpu.make_async_remote_copy(
            src_ref=gt.at[target],
            dst_ref=gx.at[me],
            send_sem=g_send.at[bits],
            recv_sem=g_recv.at[bits],
            device_id={"dp": target},
            device_id_type=MESH,
        )

    def grads(step, carry):
        slot = lax.rem(step, 2)
        for load in fetch(step, slot):
            load.wait()

        @pl.when(step < 3)
        def _():
            for load in fetch(step + 1, 1 - slot):
                load.start()

        x = jnp.dot(table[...], wbuf[slot], preferred_element_type=jnp.float32)
        target_sum = jnp.dot(hot, tbuf[slot], preferred_element_type=jnp.float32)
        scale = 0.7978845608028654
        square = x * x
        tanh = jnp.tanh(scale * (x + 0.044715 * (square * x)))
        half = 0.5 * (1.0 + tanh)
        slope = half + 0.5 * x * (1.0 - tanh * tanh) * (scale * (1.0 + 3 * 0.044715 * square))
        grad = (slope * (count * (x * half) - target_sum)).T.astype(jnp.bfloat16)
        dest = block(step)
        gt[2 * dest] = grad[:chunk]
        gt[2 * dest + 1] = grad[chunk:]

        @pl.when(step < 3)
        def _():
            sent_grad(step, 0).start()

        sent_grad(step, 1).start()
        return carry

    lax.fori_loop(0, 4, grads, 0)
    gx[me] = gt[me]

    kern = lax.dot_general(
        table[...], table[...], (((1,), (1,)), ((), ())), preferred_element_type=jnp.float32
    )
    high = kern.astype(jnp.bfloat16)
    kern_high[...] = high
    kern_low[...] = (kern - high.astype(jnp.float32)).astype(jnp.bfloat16)

    def turn(step, carry):
        at = pl.ds(pl.multiple_of(step * 256, 256), 256)
        turned[at, :] = table[:, at].T
        return carry

    lax.fori_loop(0, table.shape[1] // 256, turn, 0)
    keep_turned = pltpu.make_async_copy(turned, turned_out, local_sem.at[2])
    keep_turned.start()

    def relay(part):
        mom.arrived(0, part)
        mom.copy(2, part).start()
        mom.copy(4, part).start()
        mom.arrived(1, part + 2)
        mom.copy(2, part + 2).start()
        mom.copy(5, part + 2).start()

    def grams(bits, carry):
        source = flip(me, bits)

        @pl.when(bits > 0)
        def _():
            pltpu.make_async_remote_copy(
                src_ref=gt.at[source],
                dst_ref=gx.at[source],
                send_sem=g_send.at[bits],
                recv_sem=g_recv.at[bits],
                device_id={"dp": source},
                device_id_type=MESH,
            ).wait_recv()

        mapped[...] = jnp.dot(
            gx[source], kern_high[...], preferred_element_type=jnp.float32
        ) + jnp.dot(gx[source], kern_low[...], preferred_element_type=jnp.float32)

        def pair(other, inner_carry):
            partner = flip(me, other)
            total = jnp.sum(
                gx[partner].astype(jnp.float32) * mapped[...], axis=0, keepdims=True
            )
            sums[source, pl.ds(partner, 1), :] = total
            sums[partner, pl.ds(source, 1), :] = total
            return inner_carry

        lax.fori_loop(0, bits + 1, pair, 0)
        return carry

    lax.fori_loop(0, 7, grams, 0)
    relay(0)
    grams(7, 0)

    lanes = lax.broadcasted_iota(jnp.int32, (8, 128), 1)
    gram = jnp.zeros((8, 128), jnp.float32)
    for index in range(8):
        column = jnp.sum(sums[index], axis=1, keepdims=True)
        gram = gram + jnp.where(lanes == index, column, 0.0)
    gram, t_copies = exchange("tensor", 4, gram, t_sent, t_slots, ts_send, ts_recv, lambda: None)
    gram, d_copies = exchange(
        "dp", 8, gram, d_sent, d_slots, ds_send, ds_recv, lambda: relay(1)
    )
    coef_buf[...] = tree_columns(gram)

    for lane in range(gx.shape[2] // 128):
        at = pl.ds(lane * 128, 128)
        total = coef_buf[0:1, :] * gx[0, :, at].astype(jnp.float32)
        for index in range(1, 8):
            total = total + coef_buf[index : index + 1, :] * gx[index, :, at].astype(jnp.float32)
        mix_own[:, at] = total.astype(jnp.bfloat16)

    keep_mix = pltpu.make_async_copy(
        mix_own,
        mix_out.at[pl.ds(pl.multiple_of(me * chunk, 16), chunk)],
        local_sem.at[1],
    )
    keep_mix.start()
    mix.copy(0, 0).start()
    mix.copy(1, 1).start()
    mix.copy(0, 1).start()
    mix.copy(1, 0).start()
    for part in (0, 1):
        mix.copy(3, part).start()
    for part in (0, 1):
        mom.copy(1, part).start()
        mom.copy(0, part + 2).start()

    mix.arrived(0, 0)
    mix.copy(2, 0).start()
    mix.copy(4, 0).start()
    mix.arrived(1, 1)
    mix.copy(2, 1).start()
    mix.copy(5, 1).start()
    mix.arrived(0, 1)
    mix.copy(4, 1).start()
    mix.arrived(1, 0)
    mix.copy(5, 0).start()
    for part in range(4):
        mom.arrived(2, part)
        mom.copy(6, part).start()
    for part in (0, 1):
        mom.arrived(1, part)
        mom.copy(5, part).start()
        mom.arrived(0, part + 2)
        mom.copy(4, part + 2).start()
    for part in (0, 1):
        mix.arrived(2, part)
        mix.copy(6, part).start()

    for gather in (mom, mix):
        for part in range(gather.parts):
            for kind in (3, 4, 5, 6):
                gather.arrived(kind, part)
            for kind in range(7):
                gather.copy(kind, part).wait_send()
    for step in range(4):
        if step < 3:
            sent_grad(step, 0).wait_send()
        sent_grad(step, 1).wait_send()
    for copy in t_copies + d_copies:
        copy.wait_send()
    keep_mom.wait()
    keep_mix.wait()
    keep_turned.wait()


def mixed_grads(token_ids, table, weights, targets, momentum):
    rows, depth = table.shape
    cols = weights.shape[1]
    chunk = cols // 8
    width = 2 * chunk
    anywhere = pl.BlockSpec(memory_space=pl.ANY)
    resident = pl.BlockSpec(memory_space=pltpu.VMEM)
    dma = pltpu.SemaphoreType.DMA
    bf16, f32 = jnp.bfloat16, jnp.float32
    return pl.pallas_call(
        mix_kernel,
        out_shape=(
            jax.ShapeDtypeStruct((cols, rows), bf16),
            jax.ShapeDtypeStruct((8 * momentum.shape[0], cols), bf16),
            jax.ShapeDtypeStruct((depth, rows), bf16),
        ),
        in_specs=[resident, resident, anywhere, anywhere, anywhere],
        out_specs=(anywhere, anywhere, anywhere),
        scratch_shapes=[
            pltpu.VMEM(momentum.shape, f32),
            pltpu.VMEM(momentum.shape, bf16),
            pltpu.VMEM((depth, rows), bf16),
            pltpu.VMEM((2, depth, width), bf16),
            pltpu.VMEM((2, targets.shape[0], width), bf16),
            pltpu.VMEM((8, chunk, rows), bf16),
            pltpu.VMEM((8, chunk, rows), bf16),
            pltpu.VMEM((rows, rows), bf16),
            pltpu.VMEM((rows, rows), bf16),
            pltpu.VMEM((chunk, rows), f32),
            pltpu.VMEM((8, 8, rows), f32),
            pltpu.VMEM((8, 128), f32),
            pltpu.VMEM((chunk, rows), bf16),
            pltpu.VMEM((8, 128), f32),
            pltpu.VMEM((4, 8, 128), f32),
            pltpu.VMEM((8, 128), f32),
            pltpu.VMEM((8, 8, 128), f32),
            dma((2,)), dma((2,)), dma((4,)), dma((3,)),
            dma((7, 4)), dma((7, 4)), dma((7, 2)), dma((7, 2)),
            dma((8,)), dma((8,)), dma((4,)), dma((4,)), dma((8,)), dma((8,)),
        ],
        compiler_params=pltpu.CompilerParams(
            collective_id=0, has_side_effects=True, vmem_limit_bytes=56 * 2**20
        ),
        cost_estimate=pl.CostEstimate(
            flops=2 * rows * depth * cols, bytes_accessed=2 * depth * cols, transcendentals=0
        ),
    )(token_ids[None, :], table, weights, targets, momentum)


def update_kernel(
    turned, mix, weights, all_momentum, momentum, new_weights, new_momentum, mix_turned
):
    @pl.when(pl.program_id(0) == 0)
    def _():
        mix_turned[...] = mix[...].T

    adasum = jnp.dot(turned[...], mix_turned[...], preferred_element_type=jnp.float32)

    @pl.when(pl.program_id(0) == lax.axis_index("dp"))
    def _():
        new_momentum[...] = momentum_decay * momentum[...] + adasum

    step = momentum_decay * all_momentum[...].astype(jnp.float32) + adasum
    new_weights[...] = (weights[...].astype(jnp.float32) - learning_rate * step).astype(
        jnp.bfloat16
    )


def updated(turned, mix, weights, all_momentum, momentum):
    depth, rows = turned.shape
    owned, cols = momentum.shape

    def whole(shape):
        return pl.BlockSpec(shape, lambda step: (0, 0))

    def by_rows(width):
        return pl.BlockSpec((owned, width), lambda step: (step, 0))

    return pl.pallas_call(
        update_kernel,
        grid=(depth // owned,),
        out_shape=(
            jax.ShapeDtypeStruct((depth, cols), jnp.bfloat16),
            jax.ShapeDtypeStruct((owned, cols), jnp.float32),
        ),
        in_specs=[
            by_rows(rows),
            whole((cols, rows)),
            by_rows(cols),
            by_rows(cols),
            whole((owned, cols)),
        ],
        out_specs=(by_rows(cols), whole((owned, cols))),
        scratch_shapes=[pltpu.VMEM((rows, cols), jnp.bfloat16)],
        compiler_params=pltpu.CompilerParams(vmem_limit_bytes=56 * 2**20),
        cost_estimate=pl.CostEstimate(
            flops=2 * rows * depth * cols, bytes_accessed=6 * depth * cols, transcendentals=0
        ),
    )(turned, mix, weights, all_momentum, momentum)


def kernel_body(token_ids, table, weights, targets, momentum):
    mix, all_momentum, turned = mixed_grads(token_ids, table, weights, targets, momentum)
    return updated(turned, mix, weights, all_momentum, momentum)


def solution(mesh):
    placed = (P("dp"), P(), P(None, "tensor"), P("dp", "tensor"), P("dp", "tensor"))
    small = mesh.shape["dp"] == 8 and mesh.shape["tensor"] == 4
    return jax.shard_map(
        kernel_body if small else body,
        mesh=mesh,
        in_specs=placed,
        out_specs=(P(None, "tensor"), P("dp", "tensor")),
        check_vma=False,
    )
```

```python
import jax
import jax.numpy as jnp
from jax import lax
from jax.experimental import pallas as pl
from jax.experimental.pallas import tpu as pltpu
from jax.sharding import PartitionSpec as P

epsilon = 1e-06
momentum_decay = 0.9
learning_rate = 0.25


def gelu_tanh(values):
    return jax.nn.gelu(values, approximate=True)


def row_grads(token_ids, table, weights, targets):
    row = lax.broadcasted_iota(jnp.int32, (table.shape[0], token_ids.shape[0]), 0)
    hot = row == token_ids[None, :]
    count = jnp.sum(hot.astype(jnp.float32), axis=1, keepdims=True)
    target_sum = jnp.dot(hot.astype(jnp.bfloat16), targets, preferred_element_type=jnp.float32)
    preact = jnp.dot(table, weights, preferred_element_type=jnp.float32)
    activated, pullback = jax.vjp(gelu_tanh, preact)
    return pullback(count * activated - target_sum)[0].astype(jnp.bfloat16)


def split_kernel(table):
    kern = lax.dot_general(
        table, table, (((1,), (1,)), ((), ())), preferred_element_type=jnp.float32
    )
    high = kern.astype(jnp.bfloat16)
    return high, (kern - high.astype(jnp.float32)).astype(jnp.bfloat16)


def tree_coefficients(gram):
    replicas = gram.shape[0]
    vecs = jnp.eye(replicas, dtype=jnp.float32)
    while vecs.shape[0] > 1:
        half = vecs.shape[0] // 2
        low, high = vecs[:half], vecs[half:]
        low_g = jnp.sum(low[:, :, None] * gram[None], axis=1)
        high_g = jnp.sum(high[:, :, None] * gram[None], axis=1)
        cross = jnp.sum(low_g * high, axis=1, keepdims=True)
        low_sq = jnp.maximum(jnp.sum(low_g * low, axis=1, keepdims=True), 0.0)
        high_sq = jnp.maximum(jnp.sum(high_g * high, axis=1, keepdims=True), 0.0)
        vecs = (1.0 - cross / (2.0 * (low_sq + epsilon))) * low + (
            1.0 - cross / (2.0 * (high_sq + epsilon))
        ) * high
    return vecs[0]


def body(token_ids, table, weights, targets, momentum):
    replicas = lax.axis_size("dp")
    me = lax.axis_index("dp")
    all_momentum = lax.all_gather(momentum.astype(jnp.bfloat16), "dp", axis=0, tiled=True)
    grads = row_grads(token_ids, table, weights, targets)
    rows, cols = grads.shape
    own = lax.all_to_all(grads, "dp", split_axis=1, concat_axis=0, tiled=True)
    own = own.reshape(replicas, rows, cols // replicas)
    high, low = split_kernel(table)
    gram = []
    for other in range(replicas):
        mapped = jnp.dot(high, own[other], preferred_element_type=jnp.float32) + jnp.dot(
            low, own[other], preferred_element_type=jnp.float32
        )
        gram.append(jnp.sum(own.astype(jnp.float32) * mapped[None], axis=(1, 2)))
    gram = lax.psum(jnp.stack(gram), ("dp", "tensor"))
    coefs = tree_coefficients(gram)
    mixed = jnp.sum(own.astype(jnp.float32) * coefs[:, None, None], axis=0).astype(jnp.bfloat16)
    mixed = lax.all_gather(mixed, "dp", axis=1, tiled=True)
    adasum = lax.dot_general(
        table, mixed, (((0,), (0,)), ((), ())), preferred_element_type=jnp.float32
    )
    owned = momentum.shape[0]
    own_table = lax.dynamic_slice_in_dim(table, me * owned, owned, 1)
    own_adasum = lax.dot_general(
        own_table, mixed, (((0,), (0,)), ((), ())), preferred_element_type=jnp.float32
    )
    new_momentum = momentum_decay * momentum + own_adasum
    new_weights = (
        weights.astype(jnp.float32)
        - learning_rate * (momentum_decay * all_momentum.astype(jnp.float32) + adasum)
    ).astype(jnp.bfloat16)
    return (new_weights, new_momentum)


MESH = pl.DeviceIdType.MESH


def flip(index, bits):
    out = 0
    for place in (4, 2, 1):
        bit = lax.rem(lax.div(index, place), 2)
        out = out + place * lax.rem(bit + lax.rem(lax.div(bits, place), 2), 2)
    return out


class Gather:
    def __init__(self, me, out, send, recv, parts):
        self.me, self.out, self.send, self.recv = me, out, send, recv
        self.parts, self.piece = parts, out.shape[0] // 8
        self.rows = self.piece // parts

    def place(self, owner, part):
        start = pl.multiple_of(owner * self.piece + part * self.rows, 16)
        return self.out.at[pl.ds(start, self.rows)]

    def moved(self, kind, part):
        if kind in (0, 1, 3):
            owner, towards = 0, {0: 2, 1: 4, 3: 1}[kind]
        elif kind == 2:
            owner, towards = (2, 4) if part < self.parts // 2 else (4, 2)
        else:
            owner, towards = {4: 2, 5: 4, 6: 6}[kind], 1
        return owner, towards

    def copy(self, kind, part):
        owner, towards = self.moved(kind, part)
        here = self.place(flip(self.me, owner), part)
        return pltpu.make_async_remote_copy(
            src_ref=here,
            dst_ref=here,
            send_sem=self.send.at[kind, part],
            recv_sem=self.recv.at[kind, part],
            device_id={"dp": flip(self.me, towards)},
            device_id_type=MESH,
        )

    def arrived(self, kind, part):
        owner, towards = self.moved(kind, part)
        here = self.place(flip(self.me, owner ^ towards), part)
        pltpu.make_async_remote_copy(
            src_ref=here,
            dst_ref=here,
            send_sem=self.send.at[kind, part],
            recv_sem=self.recv.at[kind, part],
            device_id={"dp": flip(self.me, towards)},
            device_id_type=MESH,
        ).wait_recv()


def exchange(axis, size, value, sent, slots, send, recv, meanwhile):
    me = lax.axis_index(axis)
    sent[...] = value
    slots[me] = value
    copies = []
    for shift in range(1, size):
        copies.append(
            pltpu.make_async_remote_copy(
                src_ref=sent,
                dst_ref=slots.at[me],
                send_sem=send.at[shift],
                recv_sem=recv.at[shift],
                device_id={axis: lax.rem(me + shift, size)},
                device_id_type=MESH,
            )
        )
        copies[-1].start()
    meanwhile()
    for shift in range(1, size):
        origin = lax.rem(me + size - shift, size)
        pltpu.make_async_remote_copy(
            src_ref=sent,
            dst_ref=slots.at[origin],
            send_sem=send.at[shift],
            recv_sem=recv.at[shift],
            device_id={axis: origin},
            device_id_type=MESH,
        ).wait_recv()
    total = slots[0]
    for index in range(1, size):
        total = total + slots[index]
    return total, copies


def tree_columns(gram):
    rows = lax.broadcasted_iota(jnp.int32, gram.shape, 0)
    lanes = lax.broadcasted_iota(jnp.int32, (1, gram.shape[1]), 1)
    vecs = [
        ((rows == index).astype(jnp.float32), (lanes == index).astype(jnp.float32))
        for index in range(8)
    ]

    def inner(left, right):
        mapped = jnp.sum(left[0] * gram, axis=0, keepdims=True)
        return jnp.broadcast_to(jnp.sum(mapped * right[1], axis=1, keepdims=True), lanes.shape)

    while len(vecs) > 1:
        half = len(vecs) // 2
        merged = []
        for low, high in zip(vecs[:half], vecs[half:]):
            cross = inner(low, high)
            low_sq = jnp.maximum(inner(low, low), 0.0)
            high_sq = jnp.maximum(inner(high, high), 0.0)
            first = 1.0 - cross / (2.0 * (low_sq + epsilon))
            second = 1.0 - cross / (2.0 * (high_sq + epsilon))
            merged.append(
                (first * low[0] + second * high[0], first * low[1] + second * high[1])
            )
        vecs = merged
    return vecs[0][0]


def mix_kernel(
    ids, table, weights, targets, momentum, new_weights, new_momentum,
    mom_wide, mom_all, turned, wbuf, tbuf, gt, gx, kern_high, kern_low, mapped, sums, coef_buf,
    mix_all, mix_turned, wtile,
    t_sent, t_slots, d_sent, d_slots,
    w_sem, t_sem, m_sem, local_sem, load_sem, store_sem, mom_send, mom_recv, mix_send, mix_recv,
    g_send, g_recv, ts_send, ts_recv, ds_send, ds_recv,
):
    me = lax.axis_index("dp")
    mine = lax.axis_index("tensor")
    chip, core = lax.div(me, 2), lax.rem(me, 2)
    width = wbuf.shape[2]
    chunk = gt.shape[1]

    def block(step):
        return lax.div(flip(2 * chip, 2 * lax.rem(step + 1, 4)), 2)

    def fetch(step, slot):
        at = pl.ds(pl.multiple_of(block(step) * width, 128), width)
        return (
            pltpu.make_async_copy(weights.at[:, at], wbuf.at[slot], w_sem.at[slot]),
            pltpu.make_async_copy(targets.at[:, at], tbuf.at[slot], t_sem.at[slot]),
        )

    mom = Gather(me, mom_all, mom_send, mom_recv, 4)
    mix = Gather(me, mix_all, mix_send, mix_recv, 2)

    def mom_rows(part):
        return pl.ds(part * mom.rows, mom.rows)

    def mom_load(part):
        at = mom_rows(part)
        return pltpu.make_async_copy(momentum.at[at], mom_wide.at[at], m_sem.at[part])

    for part in (0, 2, 1, 3):
        mom_load(part).start()
    for load in fetch(0, 0):
        load.start()

    barrier = pltpu.get_barrier_semaphore()
    for shift in range(1, 8):
        pl.semaphore_signal(
            barrier, inc=1, device_id={"dp": lax.rem(me + shift, 8)}, device_id_type=MESH
        )
    for shift in range(1, 4):
        pl.semaphore_signal(
            barrier, inc=1, device_id={"tensor": lax.rem(mine + shift, 4)}, device_id_type=MESH
        )
    for part in (0, 2, 1, 3):
        mom_load(part).wait()
        mom_place = pl.ds(pl.multiple_of(me * mom.piece + part * mom.rows, 16), mom.rows)
        mom_all[mom_place, :] = mom_wide[mom_rows(part), :].astype(jnp.bfloat16)
    pl.semaphore_wait(barrier, 10)

    for part in (0, 1):
        mom.copy(0, part).start()
        mom.copy(1, part + 2).start()
    for part in range(4):
        mom.copy(3, part).start()

    row = lax.broadcasted_iota(jnp.int32, (table.shape[0], ids.shape[1]), 0)
    hot = (row == ids[...]).astype(jnp.float32)
    count = jnp.sum(hot, axis=1, keepdims=True)
    hot = hot.astype(jnp.bfloat16)

    def sent_grad(step, other):
        bits = 2 * lax.rem(step + 1, 4) + other
        target = flip(me, bits)
        return pltpu.make_async_remote_copy(
            src_ref=gt.at[target],
            dst_ref=gx.at[me],
            send_sem=g_send.at[bits],
            recv_sem=g_recv.at[bits],
            device_id={"dp": target},
            device_id_type=MESH,
        )

    def grads(step, carry):
        slot = lax.rem(step, 2)
        for load in fetch(step, slot):
            load.wait()

        @pl.when(step < 3)
        def _():
            for load in fetch(step + 1, 1 - slot):
                load.start()

        x = jnp.dot(table[...], wbuf[slot], preferred_element_type=jnp.float32)
        target_sum = jnp.dot(hot, tbuf[slot], preferred_element_type=jnp.float32)
        scale = 0.7978845608028654
        square = x * x
        tanh = jnp.tanh(scale * (x + 0.044715 * (square * x)))
        half = 0.5 * (1.0 + tanh)
        slope = half + 0.5 * x * (1.0 - tanh * tanh) * (scale * (1.0 + 3 * 0.044715 * square))
        grad = (slope * (count * (x * half) - target_sum)).T.astype(jnp.bfloat16)
        dest = block(step)
        gt[2 * dest] = grad[:chunk]
        gt[2 * dest + 1] = grad[chunk:]

        @pl.when(step < 3)
        def _():
            sent_grad(step, 0).start()

        sent_grad(step, 1).start()
        return carry

    lax.fori_loop(0, 4, grads, 0)
    gx[me] = gt[me]

    kern = lax.dot_general(
        table[...], table[...], (((1,), (1,)), ((), ())), preferred_element_type=jnp.float32
    )
    high = kern.astype(jnp.bfloat16)
    kern_high[...] = high
    kern_low[...] = (kern - high.astype(jnp.float32)).astype(jnp.bfloat16)

    def turn(step, carry):
        at = pl.ds(pl.multiple_of(step * 256, 256), 256)
        turned[at, :] = table[:, at].T
        return carry

    lax.fori_loop(0, table.shape[1] // 256, turn, 0)
    half = mom.piece // 2
    tasks = [(bits, 0, 2 * half) for bits in (0, 6, 1, 7)]
    tasks += [(2, 0, half), (4, half, half), (3, 0, half), (5, half, half)]
    tasks += [(2, half, half), (4, 0, half), (3, half, half), (5, 0, half)]

    def task_rows(index):
        bits, first, count_rows = tasks[index]
        return pl.ds(pl.multiple_of(flip(me, bits) * mom.piece + first, 16), count_rows)

    def tile(index):
        return wtile.at[index % 3, pl.ds(0, tasks[index][2])]

    def load(index):
        return pltpu.make_async_copy(
            weights.at[task_rows(index)], tile(index), load_sem.at[index % 3]
        )

    def store(index):
        return pltpu.make_async_copy(
            tile(index), new_weights.at[task_rows(index)], store_sem.at[index % 3]
        )

    keep_mom = pltpu.make_async_copy(mom_wide, new_momentum, local_sem.at[0])

    def update(index):
        bits, first, count_rows = tasks[index]
        rows, slot = task_rows(index), index % 3
        load(index).wait()

        def columns(step, carry):
            at = pl.ds(pl.multiple_of(step * 512, 512), 512)
            adasum = jnp.dot(
                turned[rows, :], mix_turned[:, at], preferred_element_type=jnp.float32
            )
            if bits == 0:
                moved = momentum_decay * mom_wide[:, at] + adasum
                mom_wide[:, at] = moved
            else:
                moved = momentum_decay * mom_all[rows, at].astype(jnp.float32) + adasum
            old = wtile[slot, 0:count_rows, at].astype(jnp.float32)
            wtile[slot, 0:count_rows, at] = (old - learning_rate * moved).astype(jnp.bfloat16)
            return carry

        lax.fori_loop(0, wtile.shape[2] // 512, columns, 0)
        store(index).start()
        if bits == 0:
            keep_mom.start()
        if index >= 1:
            store(index - 1).wait()
            if index + 2 < len(tasks):
                load(index + 2).start()

    for index in range(3):
        load(index).start()

    def relay(part):
        mom.arrived(0, part)
        mom.copy(2, part).start()
        mom.copy(4, part).start()
        mom.arrived(1, part + 2)
        mom.copy(2, part + 2).start()
        mom.copy(5, part + 2).start()

    def grams(bits, carry):
        source = flip(me, bits)

        @pl.when(bits > 0)
        def _():
            pltpu.make_async_remote_copy(
                src_ref=gt.at[source],
                dst_ref=gx.at[source],
                send_sem=g_send.at[bits],
                recv_sem=g_recv.at[bits],
                device_id={"dp": source},
                device_id_type=MESH,
            ).wait_recv()

        mapped[...] = jnp.dot(
            gx[source], kern_high[...], preferred_element_type=jnp.float32
        ) + jnp.dot(gx[source], kern_low[...], preferred_element_type=jnp.float32)

        def pair(other, inner_carry):
            partner = flip(me, other)
            total = jnp.sum(
                gx[partner].astype(jnp.float32) * mapped[...], axis=0, keepdims=True
            )
            sums[source, pl.ds(partner, 1), :] = total
            sums[partner, pl.ds(source, 1), :] = total
            return inner_carry

        lax.fori_loop(0, bits + 1, pair, 0)
        return carry

    lax.fori_loop(0, 7, grams, 0)
    relay(0)
    grams(7, 0)

    lanes = lax.broadcasted_iota(jnp.int32, (8, 128), 1)
    gram = jnp.zeros((8, 128), jnp.float32)
    for index in range(8):
        column = jnp.sum(sums[index], axis=1, keepdims=True)
        gram = gram + jnp.where(lanes == index, column, 0.0)
    gram, t_copies = exchange("tensor", 4, gram, t_sent, t_slots, ts_send, ts_recv, lambda: None)
    gram, d_copies = exchange(
        "dp", 8, gram, d_sent, d_slots, ds_send, ds_recv, lambda: relay(1)
    )
    coef_buf[...] = tree_columns(gram)

    own_columns = pl.ds(pl.multiple_of(me * chunk, 16), chunk)
    for lane in range(gx.shape[2] // 128):
        at = pl.ds(lane * 128, 128)
        total = coef_buf[0:1, :] * gx[0, :, at].astype(jnp.float32)
        for index in range(1, 8):
            total = total + coef_buf[index : index + 1, :] * gx[index, :, at].astype(jnp.float32)
        mix_all[own_columns, at] = total.astype(jnp.bfloat16)

    mix.copy(0, 0).start()
    mix.copy(1, 1).start()
    mix.copy(0, 1).start()
    mix.copy(1, 0).start()
    for part in (0, 1):
        mix.copy(3, part).start()
    for part in (0, 2):
        mom.arrived(2, part)
        mom.copy(6, part).start()
    mix.arrived(0, 0)
    mix.copy(2, 0).start()
    mix.copy(4, 0).start()
    mix.arrived(1, 1)
    mix.copy(2, 1).start()
    mix.copy(5, 1).start()
    for part in (0, 1):
        mom.copy(1, part).start()
        mom.copy(0, part + 2).start()
    mix.arrived(0, 1)
    mix.copy(4, 1).start()
    mix.arrived(1, 0)
    mix.copy(5, 0).start()
    for part in (1, 3):
        mom.arrived(2, part)
        mom.copy(6, part).start()
    for part in (0, 1):
        mix.arrived(2, part)
        mix.copy(6, part).start()
    for part in (0, 1):
        for kind in (3, 4, 5, 6):
            mix.arrived(kind, part)

    def turn_mix(step, carry):
        at = pl.ds(pl.multiple_of(step * 256, 256), 256)
        mix_turned[:, at] = mix_all[at, :].T
        return carry

    lax.fori_loop(0, mix_all.shape[0] // 256, turn_mix, 0)

    def forward(part):
        mom.arrived(1, part)
        mom.copy(5, part).start()
        mom.arrived(0, part + 2)
        mom.copy(4, part + 2).start()

    update(0)
    update(1)
    for part in range(4):
        mom.arrived(3, part)
    update(2)
    forward(0)
    for part in range(4):
        mom.arrived(6, part)
    update(3)
    update(4)
    update(5)
    for part in (0, 1):
        mom.arrived(4, part)
    update(6)
    for part in (2, 3):
        mom.arrived(5, part)
    update(7)
    forward(1)
    update(8)
    update(9)
    for part in (2, 3):
        mom.arrived(4, part)
    update(10)
    for part in (0, 1):
        mom.arrived(5, part)
    update(11)
    store(len(tasks) - 1).wait()

    for gather in (mom, mix):
        for part in range(gather.parts):
            for kind in range(7):
                gather.copy(kind, part).wait_send()
    for step in range(4):
        if step < 3:
            sent_grad(step, 0).wait_send()
        sent_grad(step, 1).wait_send()
    for copy in t_copies + d_copies:
        copy.wait_send()
    keep_mom.wait()


def kernel_body(token_ids, table, weights, targets, momentum):
    rows, depth = table.shape
    cols = weights.shape[1]
    chunk = cols // 8
    width = 2 * chunk
    anywhere = pl.BlockSpec(memory_space=pl.ANY)
    resident = pl.BlockSpec(memory_space=pltpu.VMEM)
    dma = pltpu.SemaphoreType.DMA
    bf16, f32 = jnp.bfloat16, jnp.float32
    return pl.pallas_call(
        mix_kernel,
        out_shape=(
            jax.ShapeDtypeStruct((depth, cols), bf16),
            jax.ShapeDtypeStruct(momentum.shape, f32),
        ),
        in_specs=[resident, resident, anywhere, anywhere, anywhere],
        out_specs=(anywhere, anywhere),
        scratch_shapes=[
            pltpu.VMEM(momentum.shape, f32),
            pltpu.VMEM((depth, cols), bf16),
            pltpu.VMEM((depth, rows), bf16),
            pltpu.VMEM((2, depth, width), bf16),
            pltpu.VMEM((2, targets.shape[0], width), bf16),
            pltpu.VMEM((8, chunk, rows), bf16),
            pltpu.VMEM((8, chunk, rows), bf16),
            pltpu.VMEM((rows, rows), bf16),
            pltpu.VMEM((rows, rows), bf16),
            pltpu.VMEM((chunk, rows), f32),
            pltpu.VMEM((8, 8, rows), f32),
            pltpu.VMEM((8, 128), f32),
            pltpu.VMEM((cols, rows), bf16),
            pltpu.VMEM((rows, cols), bf16),
            pltpu.VMEM((3, *momentum.shape), bf16),
            pltpu.VMEM((8, 128), f32),
            pltpu.VMEM((4, 8, 128), f32),
            pltpu.VMEM((8, 128), f32),
            pltpu.VMEM((8, 8, 128), f32),
            dma((2,)), dma((2,)), dma((4,)), dma((1,)), dma((3,)), dma((3,)),
            dma((7, 4)), dma((7, 4)), dma((7, 2)), dma((7, 2)),
            dma((8,)), dma((8,)), dma((4,)), dma((4,)), dma((8,)), dma((8,)),
        ],
        compiler_params=pltpu.CompilerParams(
            collective_id=0, has_side_effects=True, vmem_limit_bytes=60 * 2**20
        ),
        cost_estimate=pl.CostEstimate(
            flops=2 * rows * depth * cols, bytes_accessed=2 * depth * cols, transcendentals=0
        ),
    )(token_ids[None, :], table, weights, targets, momentum)


def solution(mesh):
    placed = (P("dp"), P(), P(None, "tensor"), P("dp", "tensor"), P("dp", "tensor"))
    small = mesh.shape["dp"] == 8 and mesh.shape["tensor"] == 4
    return jax.shard_map(
        kernel_body if small else body,
        mesh=mesh,
        in_specs=placed,
        out_specs=(P(None, "tensor"), P("dp", "tensor")),
        check_vma=False,
    )
```

```python
import jax
import jax.numpy as jnp
from jax import lax
from jax.experimental import pallas as pl
from jax.experimental.pallas import tpu as pltpu
from jax.sharding import PartitionSpec as P

epsilon = 1e-06
momentum_decay = 0.9
learning_rate = 0.25


def gelu_tanh(values):
    return jax.nn.gelu(values, approximate=True)


def row_grads(token_ids, table, weights, targets):
    row = lax.broadcasted_iota(jnp.int32, (table.shape[0], token_ids.shape[0]), 0)
    hot = row == token_ids[None, :]
    count = jnp.sum(hot.astype(jnp.float32), axis=1, keepdims=True)
    target_sum = jnp.dot(hot.astype(jnp.bfloat16), targets, preferred_element_type=jnp.float32)
    preact = jnp.dot(table, weights, preferred_element_type=jnp.float32)
    activated, pullback = jax.vjp(gelu_tanh, preact)
    return pullback(count * activated - target_sum)[0].astype(jnp.bfloat16)


def split_kernel(table):
    kern = lax.dot_general(
        table, table, (((1,), (1,)), ((), ())), preferred_element_type=jnp.float32
    )
    high = kern.astype(jnp.bfloat16)
    return high, (kern - high.astype(jnp.float32)).astype(jnp.bfloat16)


def tree_coefficients(gram):
    replicas = gram.shape[0]
    vecs = jnp.eye(replicas, dtype=jnp.float32)
    while vecs.shape[0] > 1:
        half = vecs.shape[0] // 2
        low, high = vecs[:half], vecs[half:]
        low_g = jnp.sum(low[:, :, None] * gram[None], axis=1)
        high_g = jnp.sum(high[:, :, None] * gram[None], axis=1)
        cross = jnp.sum(low_g * high, axis=1, keepdims=True)
        low_sq = jnp.maximum(jnp.sum(low_g * low, axis=1, keepdims=True), 0.0)
        high_sq = jnp.maximum(jnp.sum(high_g * high, axis=1, keepdims=True), 0.0)
        vecs = (1.0 - cross / (2.0 * (low_sq + epsilon))) * low + (
            1.0 - cross / (2.0 * (high_sq + epsilon))
        ) * high
    return vecs[0]


def body(token_ids, table, weights, targets, momentum):
    replicas = lax.axis_size("dp")
    me = lax.axis_index("dp")
    all_momentum = lax.all_gather(momentum.astype(jnp.bfloat16), "dp", axis=0, tiled=True)
    grads = row_grads(token_ids, table, weights, targets)
    rows, cols = grads.shape
    own = lax.all_to_all(grads, "dp", split_axis=1, concat_axis=0, tiled=True)
    own = own.reshape(replicas, rows, cols // replicas)
    high, low = split_kernel(table)
    gram = []
    for other in range(replicas):
        mapped = jnp.dot(high, own[other], preferred_element_type=jnp.float32) + jnp.dot(
            low, own[other], preferred_element_type=jnp.float32
        )
        gram.append(jnp.sum(own.astype(jnp.float32) * mapped[None], axis=(1, 2)))
    gram = lax.psum(jnp.stack(gram), ("dp", "tensor"))
    coefs = tree_coefficients(gram)
    mixed = jnp.sum(own.astype(jnp.float32) * coefs[:, None, None], axis=0).astype(jnp.bfloat16)
    mixed = lax.all_gather(mixed, "dp", axis=1, tiled=True)
    adasum = lax.dot_general(
        table, mixed, (((0,), (0,)), ((), ())), preferred_element_type=jnp.float32
    )
    owned = momentum.shape[0]
    own_table = lax.dynamic_slice_in_dim(table, me * owned, owned, 1)
    own_adasum = lax.dot_general(
        own_table, mixed, (((0,), (0,)), ((), ())), preferred_element_type=jnp.float32
    )
    new_momentum = momentum_decay * momentum + own_adasum
    new_weights = (
        weights.astype(jnp.float32)
        - learning_rate * (momentum_decay * all_momentum.astype(jnp.float32) + adasum)
    ).astype(jnp.bfloat16)
    return (new_weights, new_momentum)


MESH = pl.DeviceIdType.MESH


def flip(index, bits):
    out = 0
    for place in (4, 2, 1):
        bit = lax.rem(lax.div(index, place), 2)
        out = out + place * lax.rem(bit + lax.rem(lax.div(bits, place), 2), 2)
    return out


class Gather:
    def __init__(self, me, out, send, recv, parts):
        self.me, self.out, self.send, self.recv = me, out, send, recv
        self.parts, self.piece = parts, out.shape[0] // 8
        self.rows = self.piece // parts

    def place(self, owner, part):
        start = pl.multiple_of(owner * self.piece + part * self.rows, 16)
        return self.out.at[pl.ds(start, self.rows)]

    def moved(self, kind, part):
        if kind in (0, 1, 3):
            owner, towards = 0, {0: 2, 1: 4, 3: 1}[kind]
        elif kind == 2:
            owner, towards = (2, 4) if part < self.parts // 2 else (4, 2)
        else:
            owner, towards = {4: 2, 5: 4, 6: 6}[kind], 1
        return owner, towards

    def copy(self, kind, part):
        owner, towards = self.moved(kind, part)
        here = self.place(flip(self.me, owner), part)
        return pltpu.make_async_remote_copy(
            src_ref=here,
            dst_ref=here,
            send_sem=self.send.at[kind, part],
            recv_sem=self.recv.at[kind, part],
            device_id={"dp": flip(self.me, towards)},
            device_id_type=MESH,
        )

    def arrived(self, kind, part):
        owner, towards = self.moved(kind, part)
        here = self.place(flip(self.me, owner ^ towards), part)
        pltpu.make_async_remote_copy(
            src_ref=here,
            dst_ref=here,
            send_sem=self.send.at[kind, part],
            recv_sem=self.recv.at[kind, part],
            device_id={"dp": flip(self.me, towards)},
            device_id_type=MESH,
        ).wait_recv()


def exchange(axis, size, value, sent, slots, send, recv, meanwhile):
    me = lax.axis_index(axis)
    sent[...] = value
    slots[me] = value
    copies = []
    for shift in range(1, size):
        copies.append(
            pltpu.make_async_remote_copy(
                src_ref=sent,
                dst_ref=slots.at[me],
                send_sem=send.at[shift],
                recv_sem=recv.at[shift],
                device_id={axis: lax.rem(me + shift, size)},
                device_id_type=MESH,
            )
        )
        copies[-1].start()
    meanwhile()
    for shift in range(1, size):
        origin = lax.rem(me + size - shift, size)
        pltpu.make_async_remote_copy(
            src_ref=sent,
            dst_ref=slots.at[origin],
            send_sem=send.at[shift],
            recv_sem=recv.at[shift],
            device_id={axis: origin},
            device_id_type=MESH,
        ).wait_recv()
    total = slots[0]
    for index in range(1, size):
        total = total + slots[index]
    return total, copies


def tree_columns(gram):
    rows = lax.broadcasted_iota(jnp.int32, gram.shape, 0)
    lanes = lax.broadcasted_iota(jnp.int32, (1, gram.shape[1]), 1)
    vecs = [
        ((rows == index).astype(jnp.float32), (lanes == index).astype(jnp.float32))
        for index in range(8)
    ]

    def inner(left, right):
        mapped = jnp.sum(left[0] * gram, axis=0, keepdims=True)
        return jnp.broadcast_to(jnp.sum(mapped * right[1], axis=1, keepdims=True), lanes.shape)

    while len(vecs) > 1:
        half = len(vecs) // 2
        merged = []
        for low, high in zip(vecs[:half], vecs[half:]):
            cross = inner(low, high)
            low_sq = jnp.maximum(inner(low, low), 0.0)
            high_sq = jnp.maximum(inner(high, high), 0.0)
            first = 1.0 - cross / (2.0 * (low_sq + epsilon))
            second = 1.0 - cross / (2.0 * (high_sq + epsilon))
            merged.append(
                (first * low[0] + second * high[0], first * low[1] + second * high[1])
            )
        vecs = merged
    return vecs[0][0]


def mix_kernel(
    ids, table, weights, targets, momentum, new_weights, new_momentum,
    mom_wide, mom_all, turned, wbuf, tbuf, gt, gx, kern_high, kern_low, mapped, sums, coef_buf,
    mix_all, mix_turned, wtile,
    t_sent, t_slots, d_sent, d_slots,
    w_sem, t_sem, m_sem, local_sem, load_sem, store_sem, mom_send, mom_recv, mix_send, mix_recv,
    g_send, g_recv, ts_send, ts_recv, ds_send, ds_recv,
):
    me = lax.axis_index("dp")
    mine = lax.axis_index("tensor")
    chip, core = lax.div(me, 2), lax.rem(me, 2)
    width = wbuf.shape[2]
    chunk = gt.shape[1]

    def block(step):
        return lax.div(flip(2 * chip, 2 * lax.rem(step + 1, 4)), 2)

    def fetch(step, slot):
        at = pl.ds(pl.multiple_of(block(step) * width, 128), width)
        return (
            pltpu.make_async_copy(weights.at[:, at], wbuf.at[slot], w_sem.at[slot]),
            pltpu.make_async_copy(targets.at[:, at], tbuf.at[slot], t_sem.at[slot]),
        )

    mom = Gather(me, mom_all, mom_send, mom_recv, 10)
    mix = Gather(me, mix_all, mix_send, mix_recv, 2)

    def mom_rows(part):
        return pl.ds(part * mom.rows, mom.rows)

    def mom_load(part):
        at = mom_rows(part)
        return pltpu.make_async_copy(momentum.at[at], mom_wide.at[at], m_sem.at[part])

    order = (0, 5, 1, 6, 2, 7, 3, 8, 4, 9)
    for part in order:
        mom_load(part).start()
    for load in fetch(0, 0):
        load.start()

    barrier = pltpu.get_barrier_semaphore()
    for shift in range(1, 8):
        pl.semaphore_signal(
            barrier, inc=1, device_id={"dp": lax.rem(me + shift, 8)}, device_id_type=MESH
        )
    for shift in range(1, 4):
        pl.semaphore_signal(
            barrier, inc=1, device_id={"tensor": lax.rem(mine + shift, 4)}, device_id_type=MESH
        )
    for part in order:
        mom_load(part).wait()
        mom_place = pl.ds(pl.multiple_of(me * mom.piece + part * mom.rows, 16), mom.rows)
        mom_all[mom_place, :] = mom_wide[mom_rows(part), :].astype(jnp.bfloat16)
    pl.semaphore_wait(barrier, 10)

    for part in range(5):
        mom.copy(0, part).start()
        mom.copy(1, part + 5).start()
    for part in range(10):
        mom.copy(3, part).start()

    row = lax.broadcasted_iota(jnp.int32, (table.shape[0], ids.shape[1]), 0)
    hot = (row == ids[...]).astype(jnp.float32)
    count = jnp.sum(hot, axis=1, keepdims=True)
    hot = hot.astype(jnp.bfloat16)

    def sent_grad(step, other):
        bits = 2 * lax.rem(step + 1, 4) + other
        target = flip(me, bits)
        return pltpu.make_async_remote_copy(
            src_ref=gt.at[target],
            dst_ref=gx.at[me],
            send_sem=g_send.at[bits],
            recv_sem=g_recv.at[bits],
            device_id={"dp": target},
            device_id_type=MESH,
        )

    def grads(step, carry):
        slot = lax.rem(step, 2)
        for load in fetch(step, slot):
            load.wait()

        @pl.when(step < 3)
        def _():
            for load in fetch(step + 1, 1 - slot):
                load.start()

        x = jnp.dot(table[...], wbuf[slot], preferred_element_type=jnp.float32)
        target_sum = jnp.dot(hot, tbuf[slot], preferred_element_type=jnp.float32)
        scale = 0.7978845608028654
        square = x * x
        tanh = jnp.tanh(scale * (x + 0.044715 * (square * x)))
        half = 0.5 * (1.0 + tanh)
        slope = half + 0.5 * x * (1.0 - tanh * tanh) * (scale * (1.0 + 3 * 0.044715 * square))
        grad = (slope * (count * (x * half) - target_sum)).T.astype(jnp.bfloat16)
        dest = block(step)
        gt[2 * dest] = grad[:chunk]
        gt[2 * dest + 1] = grad[chunk:]

        @pl.when(step < 3)
        def _():
            sent_grad(step, 0).start()

        sent_grad(step, 1).start()
        return carry

    lax.fori_loop(0, 4, grads, 0)
    gx[me] = gt[me]

    kern = lax.dot_general(
        table[...], table[...], (((1,), (1,)), ((), ())), preferred_element_type=jnp.float32
    )
    high = kern.astype(jnp.bfloat16)
    kern_high[...] = high
    kern_low[...] = (kern - high.astype(jnp.float32)).astype(jnp.bfloat16)

    def turn(step, carry):
        at = pl.ds(pl.multiple_of(step * 256, 256), 256)
        turned[at, :] = table[:, at].T
        return carry

    lax.fori_loop(0, table.shape[1] // 256, turn, 0)
    half, early = 5 * mom.rows, 3 * mom.rows
    tasks = [(0, 0, 2 * half), (1, 0, 2 * half)]
    tasks += [(2, 0, half), (4, half, half), (3, 0, half), (5, half, half)]
    tasks += [(6, 0, 2 * half), (7, 0, 2 * half)]
    for first, size in ((0, early), (early, half - early)):
        tasks += [(2, half + first, size), (4, first, size)]
        tasks += [(3, half + first, size), (5, first, size)]

    def task_rows(index):
        bits, first, count_rows = tasks[index]
        return pl.ds(pl.multiple_of(flip(me, bits) * mom.piece + first, 16), count_rows)

    def tile(index):
        return wtile.at[index % 3, pl.ds(0, tasks[index][2])]

    def load(index):
        return pltpu.make_async_copy(
            weights.at[task_rows(index)], tile(index), load_sem.at[index % 3]
        )

    def store(index):
        return pltpu.make_async_copy(
            tile(index), new_weights.at[task_rows(index)], store_sem.at[index % 3]
        )

    keep_mom = pltpu.make_async_copy(mom_wide, new_momentum, local_sem.at[0])

    def update(index):
        bits, first, count_rows = tasks[index]
        rows, slot = task_rows(index), index % 3
        load(index).wait()

        def columns(step, carry):
            at = pl.ds(pl.multiple_of(step * 512, 512), 512)
            adasum = jnp.dot(
                turned[rows, :], mix_turned[:, at], preferred_element_type=jnp.float32
            )
            if bits == 0:
                moved = momentum_decay * mom_wide[:, at] + adasum
                mom_wide[:, at] = moved
            else:
                moved = momentum_decay * mom_all[rows, at].astype(jnp.float32) + adasum
            old = wtile[slot, 0:count_rows, at].astype(jnp.float32)
            wtile[slot, 0:count_rows, at] = (old - learning_rate * moved).astype(jnp.bfloat16)
            return carry

        lax.fori_loop(0, wtile.shape[2] // 512, columns, 0)
        store(index).start()
        if bits == 0:
            keep_mom.start()
        if index >= 1:
            store(index - 1).wait()
            if index + 2 < len(tasks):
                load(index + 2).start()

    for index in range(3):
        load(index).start()

    def relay(part):
        mom.arrived(0, part)
        mom.copy(2, part).start()
        mom.copy(4, part).start()
        mom.arrived(1, part + 5)
        mom.copy(2, part + 5).start()
        mom.copy(5, part + 5).start()

    def grams(bits, carry):
        source = flip(me, bits)

        @pl.when(bits > 0)
        def _():
            pltpu.make_async_remote_copy(
                src_ref=gt.at[source],
                dst_ref=gx.at[source],
                send_sem=g_send.at[bits],
                recv_sem=g_recv.at[bits],
                device_id={"dp": source},
                device_id_type=MESH,
            ).wait_recv()

        mapped[...] = jnp.dot(
            gx[source], kern_high[...], preferred_element_type=jnp.float32
        ) + jnp.dot(gx[source], kern_low[...], preferred_element_type=jnp.float32)

        def pair(other, inner_carry):
            partner = flip(me, other)
            total = jnp.sum(
                gx[partner].astype(jnp.float32) * mapped[...], axis=0, keepdims=True
            )
            sums[source, pl.ds(partner, 1), :] = total
            sums[partner, pl.ds(source, 1), :] = total
            return inner_carry

        lax.fori_loop(0, bits + 1, pair, 0)
        return carry

    lax.fori_loop(0, 7, grams, 0)
    relay(0)
    relay(1)
    grams(7, 0)

    lanes = lax.broadcasted_iota(jnp.int32, (8, 128), 1)
    gram = jnp.zeros((8, 128), jnp.float32)
    for index in range(8):
        column = jnp.sum(sums[index], axis=1, keepdims=True)
        gram = gram + jnp.where(lanes == index, column, 0.0)
    gram, t_copies = exchange("tensor", 4, gram, t_sent, t_slots, ts_send, ts_recv, lambda: None)
    gram, d_copies = exchange(
        "dp", 8, gram, d_sent, d_slots, ds_send, ds_recv, lambda: relay(2)
    )
    coef_buf[...] = tree_columns(gram)

    own_columns = pl.ds(pl.multiple_of(me * chunk, 16), chunk)
    for lane in range(gx.shape[2] // 128):
        at = pl.ds(lane * 128, 128)
        total = coef_buf[0:1, :] * gx[0, :, at].astype(jnp.float32)
        for index in range(1, 8):
            total = total + coef_buf[index : index + 1, :] * gx[index, :, at].astype(jnp.float32)
        mix_all[own_columns, at] = total.astype(jnp.bfloat16)

    mix.copy(0, 0).start()
    mix.copy(1, 1).start()
    mix.copy(0, 1).start()
    mix.copy(1, 0).start()
    for part in (0, 1):
        mix.copy(3, part).start()
    relay(3)
    for part in (0, 1, 5, 6):
        mom.arrived(2, part)
        mom.copy(6, part).start()
    mix.arrived(0, 0)
    mix.copy(2, 0).start()
    mix.copy(4, 0).start()
    mix.arrived(1, 1)
    mix.copy(2, 1).start()
    mix.copy(5, 1).start()
    relay(4)
    for part in range(5):
        mom.copy(1, part).start()
        mom.copy(0, part + 5).start()
    mix.arrived(0, 1)
    mix.copy(4, 1).start()
    mix.arrived(1, 0)
    mix.copy(5, 0).start()
    for part in (2, 3, 7, 8):
        mom.arrived(2, part)
        mom.copy(6, part).start()
    for part in (0, 1):
        mix.arrived(2, part)
        mix.copy(6, part).start()
    for part in (0, 1):
        for kind in (3, 4, 5, 6):
            mix.arrived(kind, part)

    def turn_mix(step, carry):
        at = pl.ds(pl.multiple_of(step * 256, 256), 256)
        mix_turned[:, at] = mix_all[at, :].T
        return carry

    lax.fori_loop(0, mix_all.shape[0] // 256, turn_mix, 0)

    def forward(part):
        mom.arrived(1, part)
        mom.copy(5, part).start()
        mom.arrived(0, part + 5)
        mom.copy(4, part + 5).start()

    def landed(kind, parts):
        for part in parts:
            mom.arrived(kind, part)

    update(0)
    landed(3, range(10))
    update(1)
    forward(0)
    update(2)
    update(3)
    forward(1)
    landed(4, range(5))
    update(4)
    landed(5, range(5, 10))
    update(5)
    for part in (4, 9):
        mom.arrived(2, part)
        mom.copy(6, part).start()
    update(6)
    forward(2)
    landed(6, range(10))
    update(7)
    update(8)
    update(9)
    forward(3)
    landed(4, range(5, 8))
    update(10)
    landed(5, range(3))
    update(11)
    forward(4)
    update(12)
    update(13)
    landed(4, range(8, 10))
    update(14)
    landed(5, range(3, 5))
    update(15)
    store(len(tasks) - 1).wait()

    for gather in (mom, mix):
        for part in range(gather.parts):
            for kind in range(7):
                gather.copy(kind, part).wait_send()
    for step in range(4):
        if step < 3:
            sent_grad(step, 0).wait_send()
        sent_grad(step, 1).wait_send()
    for copy in t_copies + d_copies:
        copy.wait_send()
    keep_mom.wait()


def kernel_body(token_ids, table, weights, targets, momentum):
    rows, depth = table.shape
    cols = weights.shape[1]
    chunk = cols // 8
    width = 2 * chunk
    anywhere = pl.BlockSpec(memory_space=pl.ANY)
    resident = pl.BlockSpec(memory_space=pltpu.VMEM)
    dma = pltpu.SemaphoreType.DMA
    bf16, f32 = jnp.bfloat16, jnp.float32
    return pl.pallas_call(
        mix_kernel,
        out_shape=(
            jax.ShapeDtypeStruct((depth, cols), bf16),
            jax.ShapeDtypeStruct(momentum.shape, f32),
        ),
        in_specs=[resident, resident, anywhere, anywhere, anywhere],
        out_specs=(anywhere, anywhere),
        scratch_shapes=[
            pltpu.VMEM(momentum.shape, f32),
            pltpu.VMEM((depth, cols), bf16),
            pltpu.VMEM((depth, rows), bf16),
            pltpu.VMEM((2, depth, width), bf16),
            pltpu.VMEM((2, targets.shape[0], width), bf16),
            pltpu.VMEM((8, chunk, rows), bf16),
            pltpu.VMEM((8, chunk, rows), bf16),
            pltpu.VMEM((rows, rows), bf16),
            pltpu.VMEM((rows, rows), bf16),
            pltpu.VMEM((chunk, rows), f32),
            pltpu.VMEM((8, 8, rows), f32),
            pltpu.VMEM((8, 128), f32),
            pltpu.VMEM((cols, rows), bf16),
            pltpu.VMEM((rows, cols), bf16),
            pltpu.VMEM((3, *momentum.shape), bf16),
            pltpu.VMEM((8, 128), f32),
            pltpu.VMEM((4, 8, 128), f32),
            pltpu.VMEM((8, 128), f32),
            pltpu.VMEM((8, 8, 128), f32),
            dma((2,)), dma((2,)), dma((10,)), dma((1,)), dma((3,)), dma((3,)),
            dma((7, 10)), dma((7, 10)), dma((7, 2)), dma((7, 2)),
            dma((8,)), dma((8,)), dma((4,)), dma((4,)), dma((8,)), dma((8,)),
        ],
        compiler_params=pltpu.CompilerParams(
            collective_id=0, has_side_effects=True, vmem_limit_bytes=60 * 2**20
        ),
        cost_estimate=pl.CostEstimate(
            flops=2 * rows * depth * cols, bytes_accessed=2 * depth * cols, transcendentals=0
        ),
    )(token_ids[None, :], table, weights, targets, momentum)


def solution(mesh):
    placed = (P("dp"), P(), P(None, "tensor"), P("dp", "tensor"), P("dp", "tensor"))
    small = mesh.shape["dp"] == 8 and mesh.shape["tensor"] == 4
    return jax.shard_map(
        kernel_body if small else body,
        mesh=mesh,
        in_specs=placed,
        out_specs=(P(None, "tensor"), P("dp", "tensor")),
        check_vma=False,
    )
```
